128 devices in a mesh: dp: 32 (over y, x, z_lo), tensor: 4 (over z_hi, core).
Axes of the slice: x: 4, y: 4, z: 4 (z_hi: 2, z_lo: 2; z = z_hi * 2 + z_lo), core: 2. Of those that a mesh axis runs over, the one named last changes fastest.
Arguments:
- tokens: bfloat16 [16384, 1024], P(('dp', 'tensor')), may hold values from -6 to 6
- cotangent: bfloat16 [16384, 1024], P(('dp', 'tensor')), may hold values from -6 to 6
- norm1_gain: bfloat16 [1024], P('dp'), may hold values from 0.25 to 1.75
- w_query: bfloat16 [1024, 1024], P('dp', 'tensor'), may hold values from -0.1875 to 0.1875
- w_key: bfloat16 [1024, 512], P('dp', 'tensor'), may hold values from -0.1875 to 0.1875
- w_value: bfloat16 [1024, 512], P('dp', 'tensor'), may hold values from -0.1875 to 0.1875
- w_out: bfloat16 [1024, 1024], P('dp', 'tensor'), may hold values from -0.75 to 0.75
- norm2_gain: bfloat16 [1024], P('dp'), may hold values from 0.25 to 1.75
- expert_gate: bfloat16 [32, 1024, 512], P('dp', None, 'tensor'), may hold values from -0.1875 to 0.1875
- expert_up: bfloat16 [32, 1024, 512], P('dp', None, 'tensor'), may hold values from -0.1875 to 0.1875
- expert_down: bfloat16 [32, 512, 1024], P('dp', 'tensor'), may hold values from -0.25 to 0.25
- route_gates: float32 [16384, 8], P('dp'), may hold values from 0.15 to 0.6
- routes: int32 [16384, 8], P('dp'), may hold values from 0 to 31, all different within a row; in each aligned block of 512 rows (0 to 511, 512 to 1023, ...) at most 160 rows name the same one
- segment: int32 [16384], P('dp'), may hold values from 0 to 2, as said below
Outputs:
- output: float32 [16384, 1024], P(('dp', 'tensor'))
- grad_tokens: float32 [16384, 1024], P(('dp', 'tensor'))
- grad_norm1_gain: float32 [1024], P(('dp', 'tensor'))
- grad_w_query: float32 [1024, 1024], P('dp', 'tensor')
- grad_w_key: float32 [1024, 512], P('dp', 'tensor')
- grad_w_value: float32 [1024, 512], P('dp', 'tensor')
- grad_w_out: float32 [1024, 1024], P('dp', 'tensor')
- grad_norm2_gain: float32 [1024], P(('dp', 'tensor'))
- grad_expert_gate: float32 [32, 1024, 512], P('dp', None, 'tensor')
- grad_expert_up: float32 [32, 1024, 512], P('dp', None, 'tensor')
- grad_expert_down: float32 [32, 512, 1024], P('dp', 'tensor')
The draws below stay inside these ranges and needn't reach their ends.
Inputs may be any that keep to these rules, and one draw needn't show every extreme that they name: `segment`: each group of 512 rows holds 3 documents numbered 0, 1, 2 in order; the first and the last hold 1 to 64 rows each. `routes`: the 8 experts of a row are distinct; within each group of 512 rows no expert is named by more than 160 rows, and one is named by exactly 160.
All inputs are finite; a program needn't handle non-finite values.
Results may differ from the reference program's by a relative error of at most 0.035.
Values may be sent and summed in bfloat16 or wider, within the bound.
No kernel may reach another device: no remote copies, remote signals or barrier semaphores. Data moves between devices by JAX's collectives and lax.ppermute only.
A program may use at most 192 MiB of HBM per device.

```python
import math
import jax
import jax.numpy as jnp
import numpy as np
from jax import lax

D = 1024
H = 16
KV = 8
HD = 64
FFE = 512
EXPERTS = 32
TOPK = 8
TOK_DEV = 128
DOCS = 3
GROUP = 512
TOKENS = 16384
CAP = 160
N_TENSOR = 4


def draw_segment(key, part):
    key = jax.random.fold_in(key, 11)
    groups = TOKENS // GROUP
    head_key, tail_key = jax.random.split(key)
    head = jax.random.randint(head_key, (groups, 1), 1, TOK_DEV // 2 + 1)
    tail = jax.random.randint(tail_key, (groups, 1), GROUP - TOK_DEV // 2, GROUP)
    index = jnp.arange(GROUP, dtype=jnp.int32)[None, :]
    marks = (index >= head).astype(jnp.int32) + (index >= tail).astype(jnp.int32)
    return marks.reshape(TOKENS).astype(jnp.int32)


def shard_levels(own_key, dims, shards, smallest, high):
    loudness, own = 1.0, jax.random.fold_in(own_key, 6)
    for dim, parts in shards:
        heights = jnp.exp(jax.random.uniform(jax.random.fold_in(own, dim), (parts,), jnp.float32, smallest / len(shards), high / len(shards)))
        loudness = loudness * jnp.repeat(heights, dims[dim] // parts).reshape([-1 if axis == dim else 1 for axis in range(len(dims))])
    return loudness


def routed_block(rng, own, number, rows, amount, top, limit, skew):
    ranking = jax.random.permutation(rng, amount)
    heavy_load, usual = shares(amount, rows * top, limit, skew, True), shares(amount, rows * top, limit, skew, False)
    places = jnp.arange(amount)

    def named(tallies, offset_by):
        used = int((tallies > 0).sum())
        fixed = max(1, used // 4)
        shifted = fixed + (places - fixed + offset_by * (used - fixed)) % max(1, amount - fixed)
        return jnp.zeros((amount,), jnp.int32).at[ranking[jnp.where(places < fixed, places, shifted)]].set(jnp.asarray(tallies, jnp.int32))

    tallies = jnp.where(number % 4 == 0, named(heavy_load, number // 4), named(usual, number - number // 4 - 1))
    mixed = jax.random.permutation(jax.random.fold_in(own, 3), amount)
    giver, receiver = mixed[0:amount // 2 * 2:2], mixed[1:amount // 2 * 2:2]
    slack = jnp.minimum(tallies[giver] - 1, limit - tallies[receiver]) // 2
    slack = jnp.where((giver == ranking[0]) | (receiver == ranking[0]) | (tallies[receiver] == 0), 0, jnp.maximum(slack, 0))
    shifted = jax.random.randint(jax.random.fold_in(own, 4), (amount // 2,), 0, 1 << 20) % (slack + 1)
    tallies = tallies.at[giver].add(-shifted).at[receiver].add(shifted)
    items = jnp.searchsorted(jnp.cumsum(tallies), jnp.arange(rows * top), side="right").astype(jnp.int32)
    table = items.reshape(top, rows).T
    table = table[jax.random.permutation(jax.random.fold_in(own, 1), rows)]
    offset_by = jax.random.randint(jax.random.fold_in(own, 2), (rows, 1), 0, top)
    return jnp.take_along_axis(table, (jnp.arange(top)[None, :] + offset_by) % top, axis=1)


def shares(count, total, reach, lean, full):
    loads = [(1 << 20) // math.isqrt(rank ** lean) + 1 for rank in range(1, count + 1)]
    largest = reach if full else min(reach, max(-(-total // count), total * loads[0] // sum(loads)))
    least = 1 if total - largest >= count - 1 else 0
    given, spare = [largest] + [least] * (count - 1), total - largest - least * (count - 1)
    while spare > 0:
        movable = [i for i in range(1, count) if given[i] < largest] or [i for i in range(1, count) if given[i] < reach]
        mass, remaining = sum([loads[i] for i in movable]), spare
        for i in movable:
            addition = min(reach - given[i], max(1, remaining * loads[i] // mass), spare)
            given[i] = given[i] + addition
            spare = spare - addition
    return np.array(given)


def normal_values(own_key, dims, scale, most, cuts=(), kind=jnp.bfloat16):
    loudness = shard_levels(own_key, dims, cuts, -0.22, 0.18) if cuts else 1.0
    drawn = jax.random.normal(own_key, dims, jnp.float32) * scale * loudness
    return jnp.minimum(jnp.maximum(drawn, -most), most).astype(kind)


def setup_inputs(seed: int = 0) -> dict:
    splits = jax.random.split(jax.random.key(seed), 15)
    tokens = normal_values(splits[0], (TOKENS, D), 1.0, 6.0, ((0, 128),))
    cotangent = normal_values(splits[1], (TOKENS, D), 1.0, 6.0, ((0, 128),))
    norm1_gain = jnp.clip(1.0 + 0.15 * jax.random.normal(splits[2], (D,), jnp.float32), 0.25, 1.75).astype(jnp.bfloat16)
    w_query = normal_values(splits[3], (D, H * HD), D ** -0.5, 0.1875, ((0, 32), (1, 4)))
    w_key = normal_values(splits[4], (D, KV * HD), D ** -0.5, 0.1875, ((0, 32), (1, 4)))
    w_value = normal_values(splits[5], (D, KV * HD), D ** -0.5, 0.1875, ((0, 32), (1, 4)))
    w_out = normal_values(splits[6], (D, H * HD), (D // 16) ** -0.5, 0.75, ((0, 32), (1, 4)))
    norm2_gain = jnp.clip(1.0 + 0.15 * jax.random.normal(splits[7], (D,), jnp.float32), 0.25, 1.75).astype(jnp.bfloat16)
    expert_gate = normal_values(splits[8], (EXPERTS, D, FFE), D ** -0.5, 0.1875, ((0, 32), (2, 4)))
    expert_up = normal_values(splits[9], (EXPERTS, D, FFE), D ** -0.5, 0.1875, ((0, 32), (2, 4)))
    expert_down = normal_values(splits[10], (EXPERTS, FFE, D), FFE ** -0.5, 0.25, ((0, 32), (1, 4)))
    route_gates = jnp.clip(jnp.exp(math.log(0.6) - 1.3862944 * jax.random.uniform(splits[11], (TOKENS, TOPK), jnp.float32) ** shard_levels(splits[11], (TOKENS, TOPK), ((0, 32),), -0.2, 0.2)), 0.15, 0.6)
    routes_keys = jax.random.split(jax.random.fold_in(splits[12], 1), TOKENS // GROUP)
    routes_turns = jax.random.permutation(jax.random.fold_in(splits[12], 3), TOKENS // GROUP)
    routes = jax.vmap(lambda own, number: routed_block(jax.random.fold_in(splits[12], 2), own, number, GROUP, EXPERTS, TOPK, CAP, 1))(routes_keys, routes_turns).reshape((TOKENS, TOPK))
    segment = draw_segment(jax.random.fold_in(splits[14], 71), 0)
    return {"tokens": tokens, "cotangent": cotangent, "norm1_gain": norm1_gain, "w_query": w_query, "w_key": w_key, "w_value": w_value, "w_out": w_out, "norm2_gain": norm2_gain, "expert_gate": expert_gate, "expert_up": expert_up, "expert_down": expert_down, "route_gates": route_gates, "routes": routes, "segment": segment}


@jax.custom_vjp
def low(v):
    return lax.optimization_barrier(v.astype(jnp.bfloat16)).astype(jnp.float32)

@jax.custom_vjp
def low_back(v):
    return v

def low_keep(v):
    return (low(v), None)

def low_pass(kept, grad):
    return (grad,)

def back_keep(v):
    return (v, None)

def back_low(kept, grad):
    return (low(grad),)
low.defvjp(low_keep, low_pass)
low_back.defvjp(back_keep, back_low)
EPS = 1e-06
THETA = 10000.0
HIGHEST = lax.Precision.HIGHEST

def rms_scaled(rows, gain):
    inverse = lax.rsqrt(lax.optimization_barrier(jnp.mean(rows * rows, axis=1, keepdims=True)) + EPS)
    return rows * inverse * gain[None, :]

def doc_positions(segment):
    onehot = (segment[:, None] == jnp.arange(DOCS, dtype=jnp.int32)[None, :]).astype(jnp.int32)
    counts = lax.optimization_barrier(jnp.sum(onehot, axis=0))
    starts = jnp.cumsum(counts) - counts
    first = lax.optimization_barrier(jnp.sum(onehot * starts[None, :], axis=1))
    return (jnp.arange(segment.shape[0], dtype=jnp.int32) - first).astype(jnp.int32)

def rope_tables(segment, size):
    places = doc_positions(segment).astype(jnp.float32)
    freqs = THETA ** (-(jnp.arange(size // 2, dtype=jnp.float32) * 2.0) / size)
    angle = places[:, None] * freqs[None, :]
    return (jnp.cos(angle), jnp.sin(angle))

def rotate(values, cosine, sine, heads):
    split = values.reshape(values.shape[0], heads, 2, -1)
    first = split[:, :, 0]
    second = split[:, :, 1]
    cos_b = cosine[:, None, :]
    sin_b = sine[:, None, :]
    turned = jnp.stack([first * cos_b - second * sin_b, second * cos_b + first * sin_b], axis=2)
    return turned.reshape(values.shape)

def slot_targets(route_rows):
    flat = route_rows.reshape(-1).astype(jnp.int32)
    onehot = (flat[:, None] == jnp.arange(EXPERTS, dtype=jnp.int32)[None, :]).astype(jnp.int32)
    slot = lax.optimization_barrier(jnp.sum((jnp.cumsum(onehot, axis=0) - 1) * onehot, axis=1))
    return (flat * CAP + slot).astype(jnp.int32)

def layer_group(rows, segment, gates, route_rows, gain1, wq, wk, wv, wo, gain2, wg, wu, wd):
    group = rows.shape[0]
    ratio = H // KV
    scale = HD ** (-0.5)
    normed1 = low(rms_scaled(rows, gain1))
    cosine, sine = rope_tables(segment, HD)
    queries = low(rotate(low_back(jnp.dot(normed1, wq, precision=HIGHEST, preferred_element_type=jnp.float32)), cosine, sine, H))
    queries = queries.reshape(group, KV, ratio, HD)
    keys = low(rotate(low_back(jnp.dot(normed1, wk, precision=HIGHEST, preferred_element_type=jnp.float32)), cosine, sine, KV))
    keys = keys.reshape(group, KV, HD)
    values = low(low_back(jnp.dot(normed1, wv, precision=HIGHEST, preferred_element_type=jnp.float32))).reshape(group, KV, HD)
    block = min(512, group)
    key_index = jnp.arange(group, dtype=jnp.int32)

    def one_block(start):
        qpart = lax.dynamic_slice_in_dim(queries, start, block, 0)
        qseg = lax.dynamic_slice_in_dim(segment, start, block, 0)
        qidx = start + jnp.arange(block, dtype=jnp.int32)
        allowed = (qseg[:, None] == segment[None, :]) & (key_index[None, :] <= qidx[:, None])
        scores = low_back(jnp.einsum('qkrd,skd->krqs', qpart, keys, precision=HIGHEST) * scale)
        scores = jnp.where(allowed[None, None], scores, -1e+30)
        top = lax.optimization_barrier(jnp.max(scores, axis=3, keepdims=True))
        weights = jnp.exp(scores - top)
        probs = low(weights / lax.optimization_barrier(jnp.sum(weights, axis=3, keepdims=True)))
        return jnp.einsum('krqs,skd->qkrd', probs, values, precision=HIGHEST)
    starts = jnp.arange(group // block, dtype=jnp.int32) * block
    outs = lax.map(jax.checkpoint(one_block), starts)
    attended = low(low_back(outs.reshape(group, H * HD)))
    branch = low_back(jnp.dot(attended, wo.T, precision=HIGHEST, preferred_element_type=jnp.float32))
    mixed = rows + branch
    normed2 = low(rms_scaled(mixed, gain2))
    dest = slot_targets(route_rows)
    packed = jnp.zeros((EXPERTS * CAP, D), jnp.float32).at[dest].set(jnp.repeat(normed2, TOPK, axis=0))
    packed = packed.reshape(EXPERTS, CAP, D)
    quarter = FFE // N_TENSOR
    total = jnp.zeros((EXPERTS, CAP, D), jnp.float32)
    for part in range(N_TENSOR):
        lo_unit = part * quarter
        packed_part = low_back(packed)
        gate_pre = low_back(jnp.einsum('ecd,edf->ecf', packed_part, wg[:, :, lo_unit:lo_unit + quarter], precision=HIGHEST))
        up_pre = low_back(jnp.einsum('ecd,edf->ecf', packed_part, wu[:, :, lo_unit:lo_unit + quarter], precision=HIGHEST))
        hidden = low(jax.nn.silu(gate_pre) * up_pre)
        produced = jnp.einsum('ecf,efd->ecd', hidden, wd[:, lo_unit:lo_unit + quarter, :], precision=HIGHEST)
        total = total + low(low_back(produced))
    picked = total.reshape(EXPERTS * CAP, D)[dest].reshape(group, TOPK, D)
    return mixed + lax.optimization_barrier(jnp.sum(picked * gates[:, :, None], axis=1))

def reference(tokens, cotangent, norm1_gain, w_query, w_key, w_value, w_out, norm2_gain, expert_gate, expert_up, expert_down, route_gates, routes, segment):
    groups = TOKENS // GROUP
    params = tuple((p.astype(jnp.float32) for p in (tokens, norm1_gain, w_query, w_key, w_value, w_out, norm2_gain, expert_gate, expert_up, expert_down)))
    seg_groups = segment.reshape(groups, GROUP)
    gate_groups = route_gates.reshape(groups, GROUP, TOPK)
    route_groups = routes.reshape(groups, GROUP, TOPK)

    def forward(rows, gain1, wq, wk, wv, wo, gain2, wg, wu, wd):

        def one_group(carry, item):
            row_g, seg_g, gate_g, route_g = item
            return (carry, layer_group(row_g, seg_g, gate_g, route_g, gain1, wq, wk, wv, wo, gain2, wg, wu, wd))
        _, outs = lax.scan(jax.checkpoint(one_group), jnp.zeros((), jnp.float32), (rows.reshape(groups, GROUP, D), seg_groups, gate_groups, route_groups))
        return outs.reshape(TOKENS, D)
    output, pullback = jax.vjp(forward, *params)
    grads = pullback(cotangent.astype(jnp.float32))
    return (output, grads[0], grads[1], grads[2], grads[3], grads[4], grads[5], grads[6], grads[7], grads[8], grads[9])
```

```python
import jax
import jax.numpy as jnp
from jax import lax
from jax.sharding import PartitionSpec as P

HD = 64
DOCS = 3
EPS = 1e-06
THETA = 10000.0
BF = jnp.bfloat16
F32 = jnp.float32


def dot(a, b, dims):
    return lax.dot_general(a, b, (dims, ((), ())), preferred_element_type=F32)


def swap(x, mask):
    count = lax.axis_size("tensor")
    return lax.ppermute(x, "tensor", [(i, i ^ mask) for i in range(count)])


def gather_rel(x):
    far = swap(x, 2)
    near = swap(x, 1)
    far_near = swap(far, 1)
    return [x, near, far, far_near]


def scatter_rel(blocks):
    got = swap(jnp.stack([blocks[1], blocks[3]]).astype(BF), 1)
    mine = blocks[0].astype(F32) + got[0].astype(F32)
    other = (blocks[2].astype(F32) + got[1].astype(F32)).astype(BF)
    return mine + swap(other, 2).astype(F32)


def sum_tensor(x):
    x = x + swap(x, 1)
    return x + swap(x, 2)


def exchange(x):
    return lax.all_to_all(x, "dp", split_axis=0, concat_axis=0, tiled=True)


def gather_dp(x):
    count = lax.axis_size("dp")
    out = exchange(jnp.broadcast_to(x[None], (count,) + x.shape))
    return out.reshape(count * x.shape[0], x.shape[1])


def scatter_dp(x):
    count = lax.axis_size("dp")
    parts = exchange(x.reshape(count, x.shape[0] // count, x.shape[1]))
    return jnp.sum(parts.astype(F32), axis=0)


def rms_forward(rows):
    inverse = lax.rsqrt(jnp.mean(rows * rows, axis=1, keepdims=True) + EPS)
    return (rows * inverse, inverse)


def doc_positions(segment, index):
    onehot = (segment[:, None] == jnp.arange(DOCS, dtype=jnp.int32)[None, :]).astype(jnp.int32)
    counts = jnp.sum(onehot, axis=0)
    starts = jnp.cumsum(counts) - counts
    first = jnp.sum(onehot * starts[None, :], axis=1)
    return index - first


def rotate(values, cosine, sine, heads):
    half = HD // 2
    out = []
    for h in range(heads):
        first = values[:, h * HD : h * HD + half]
        second = values[:, h * HD + half : (h + 1) * HD]
        out.append(first * cosine - second * sine)
        out.append(second * cosine + first * sine)
    return jnp.concatenate(out, axis=1)


def on_device(
    tokens,
    cotangent,
    norm1_gain,
    w_query,
    w_key,
    w_value,
    w_out,
    norm2_gain,
    expert_gate,
    expert_up,
    expert_down,
    route_gates,
    routes,
    segment,
):
    group = segment.shape[0]
    local, width = tokens.shape
    top_k = routes.shape[1]
    dp_count = lax.axis_size("dp")
    tensor_count = lax.axis_size("tensor")
    experts = expert_gate.shape[0] * dp_count
    capacity = min(group, group * top_k * 5 // (4 * experts))
    share = capacity // tensor_count
    slots = experts * share
    piece = width // dp_count
    here = lax.axis_index("tensor")
    scale = HD ** (-0.5)
    qc, kc, vc, oc = w_query.shape[1], w_key.shape[1], w_value.shape[1], w_out.shape[1]
    heads = qc // HD
    kv_heads = kc // HD
    ratio = heads // kv_heads

    qkv_full = gather_dp(jnp.concatenate([w_query, w_key, w_value], axis=1))
    gains = jnp.stack([norm1_gain, norm2_gain], axis=1)
    gains = jnp.pad(gains, ((0, 0), (0, 128 - 2)))
    rest_full = gather_dp(jnp.concatenate([w_out, gains], axis=1))
    wo = rest_full[:, :oc]
    gain1 = rest_full[:, oc].astype(F32)
    gain2 = rest_full[:, oc + 1].astype(F32)

    blocks = jnp.arange(tensor_count, dtype=jnp.int32) ^ here
    index = (blocks[:, None] * local + jnp.arange(local, dtype=jnp.int32)[None, :]).reshape(group)

    def reorder(x):
        split = x.reshape((tensor_count, local) + x.shape[1:])
        return jnp.concatenate(
            [lax.dynamic_index_in_dim(split, here ^ s, 0, False) for s in range(tensor_count)]
        )

    seg = reorder(segment)
    route_rows = reorder(routes)
    gate_rows = reorder(route_gates)
    rows = jnp.concatenate(gather_rel(tokens)).astype(F32)
    cot_rows = jnp.concatenate(gather_rel(cotangent))

    expert_ids = jnp.arange(experts, dtype=jnp.int32)
    hit = route_rows[None, :, :] == expert_ids[:, None, None]
    member = jnp.any(hit, axis=2)
    gate_of = jnp.sum(jnp.where(hit, gate_rows[None], 0.0), axis=2)
    before = (index[:, None] < index[None, :]).astype(BF)
    slot = dot(member.astype(BF), before, ((1,), (0,)))
    slot = jnp.where(member, slot, -1.0).astype(jnp.int32)
    wanted = here * share + jnp.arange(share, dtype=jnp.int32)
    place = slot[:, None, :] == wanted[None, :, None]
    slot_gate = jnp.sum(jnp.where(place, gate_of[:, None, :], 0.0), axis=2).reshape(slots)
    place = place.astype(BF).reshape(slots, group)

    grad_packed = (dot(place, cot_rows, ((1,), (0,))) * slot_gate[:, None]).astype(BF)
    grad_arrived = exchange(grad_packed.reshape(experts, share, width)).reshape(slots, width)

    normal1, inverse1 = rms_forward(rows)
    normed1 = (normal1 * gain1[None, :]).astype(BF)
    places = doc_positions(seg, index).astype(F32)
    freqs = THETA ** (-(jnp.arange(HD // 2, dtype=F32) * 2.0) / HD)
    angle = places[:, None] * freqs[None, :]
    cosine, sine = jnp.cos(angle), jnp.sin(angle)
    projected = dot(normed1, qkv_full, ((1,), (0,)))
    queries = rotate(projected[:, :qc], cosine, sine, heads).astype(BF)
    keys = rotate(projected[:, qc : qc + kc], cosine, sine, kv_heads).astype(BF)
    values = projected[:, qc + kc :].astype(BF)
    queries = queries.reshape(group, kv_heads, ratio, HD)
    keys = keys.reshape(group, kv_heads, HD)
    values = values.reshape(group, kv_heads, HD)
    allowed = (seg[:, None] == seg[None, :]) & (index[None, :] <= index[:, None])
    scores = jnp.einsum("qkrd,skd->krqs", queries, keys, preferred_element_type=F32) * scale
    scores = jnp.where(allowed[None, None], scores, -1e30)
    top = jnp.max(scores, axis=3, keepdims=True)
    weights = jnp.exp(scores - top)
    probs = weights / jnp.sum(weights, axis=3, keepdims=True)
    probs_low = probs.astype(BF)
    attended = jnp.einsum("krqs,skd->qkrd", probs_low, values, preferred_element_type=F32)
    attended = attended.astype(BF).reshape(group, qc)
    partial = dot(attended, wo, ((1,), (1,))).astype(BF).reshape(tensor_count, local, width)
    mixed = tokens.astype(F32) + scatter_rel(partial)

    normal2, inverse2 = rms_forward(mixed)
    normed2 = (normal2 * gain2[None, :]).astype(BF)
    normed2_rows = jnp.concatenate(gather_rel(normed2))
    packed = dot(place, normed2_rows, ((1,), (0,))).astype(BF)
    arrived = exchange(packed.reshape(experts, share, width)).reshape(slots, width)

    wg = jnp.concatenate(gather_rel(expert_gate[0]), axis=1)
    wu = jnp.concatenate(gather_rel(expert_up[0]), axis=1)
    wd = jnp.concatenate(gather_rel(expert_down[0]), axis=0)
    gate_pre = dot(arrived, wg, ((1,), (0,)))
    up_pre = dot(arrived, wu, ((1,), (0,)))
    sigma = jax.nn.sigmoid(gate_pre)
    silu = gate_pre * sigma
    hidden = (silu * up_pre).astype(BF)
    grad_hidden = dot(grad_arrived, wd, ((1,), (1,)))
    grad_gate_pre = (grad_hidden * up_pre * sigma * (1.0 + gate_pre * (1.0 - sigma))).astype(BF)
    grad_up_pre = (grad_hidden * silu).astype(BF)
    grad_inputs = (
        dot(grad_gate_pre, wg, ((1,), (1,))) + dot(grad_up_pre, wu, ((1,), (1,)))
    ).astype(BF)
    grad_back = exchange(grad_inputs.reshape(experts, share, width)).reshape(slots, width)
    produced = dot(hidden, wd, ((1,), (0,))).astype(BF)
    returned = exchange(produced.reshape(experts, share, width)).reshape(slots, width)
    grad_down = dot(hidden, grad_arrived, ((0,), (0,)))
    grad_gate = dot(arrived, grad_gate_pre, ((0,), (0,)))
    grad_up = dot(arrived, grad_up_pre, ((0,), (0,)))
    units = expert_gate.shape[2]
    grad_gate = scatter_rel([grad_gate[:, s * units : (s + 1) * units] for s in range(tensor_count)])
    grad_up = scatter_rel([grad_up[:, s * units : (s + 1) * units] for s in range(tensor_count)])
    grad_down = scatter_rel([grad_down[s * units : (s + 1) * units] for s in range(tensor_count)])

    weighted = (returned.astype(F32) * slot_gate[:, None]).astype(BF)
    moe = dot(place, weighted, ((0,), (0,))).astype(BF)
    output = mixed + scatter_rel(moe.reshape(tensor_count, local, width))

    grad_normed2 = dot(place, grad_back, ((0,), (0,))).astype(BF)
    grad_normed2 = scatter_rel(grad_normed2.reshape(tensor_count, local, width))
    scaled = grad_normed2 * gain2[None, :]
    inner = jnp.mean(scaled * normal2, axis=1, keepdims=True)
    grad_mixed = cotangent.astype(F32) + inverse2 * (scaled - normal2 * inner)
    gain2_part = sum_tensor(jnp.sum(grad_normed2 * normal2, axis=0, keepdims=True))
    grad_branch = jnp.concatenate(gather_rel(grad_mixed.astype(BF)))

    grad_wo = dot(grad_branch, attended, ((0,), (0,)))
    grad_attended = dot(grad_branch, wo, ((1,), (0,))).astype(BF)
    grad_attended = grad_attended.reshape(group, kv_heads, ratio, HD)
    grad_probs = jnp.einsum("qkrd,skd->krqs", grad_attended, values, preferred_element_type=F32)
    inner = jnp.sum(probs * grad_probs, axis=3, keepdims=True)
    grad_scores = (probs * (grad_probs - inner)).astype(BF)
    grad_q = jnp.einsum("krqs,skd->qkrd", grad_scores, keys, preferred_element_type=F32) * scale
    grad_k = jnp.einsum("krqs,qkrd->skd", grad_scores, queries, preferred_element_type=F32) * scale
    grad_v = jnp.einsum("krqs,qkrd->skd", probs_low, grad_attended, preferred_element_type=F32)
    grad_q = rotate(grad_q.reshape(group, qc), cosine, -sine, heads).astype(BF)
    grad_k = rotate(grad_k.reshape(group, kc), cosine, -sine, kv_heads).astype(BF)
    grad_qkv = jnp.concatenate([grad_q, grad_k, grad_v.reshape(group, vc).astype(BF)], axis=1)
    grad_w = dot(normed1, grad_qkv, ((0,), (0,)))
    grad_normed1 = dot(grad_qkv, qkv_full, ((1,), (1,)))
    gain1_part = sum_tensor(jnp.sum(grad_normed1 * normal1, axis=0, keepdims=True))
    grad_normed1 = scatter_rel(grad_normed1.astype(BF).reshape(tensor_count, local, width))
    scaled = grad_normed1 * gain1[None, :]
    inner = jnp.mean(scaled * normal1[:local], axis=1, keepdims=True)
    grad_tokens = grad_mixed + inverse1[:local] * (scaled - normal1[:local] * inner)

    def with_gain(grads, gain_part):
        column = jnp.pad(gain_part.reshape(width, 1), ((0, 0), (0, 127)))
        return jnp.concatenate([grads, column], axis=1).astype(BF)

    wo_sum = scatter_dp(with_gain(grad_wo, gain2_part))
    w_sum = scatter_dp(with_gain(grad_w, gain1_part))
    own = piece // tensor_count
    gain2_grad = lax.dynamic_slice_in_dim(wo_sum[:, oc], here * own, own, 0)
    gain1_grad = lax.dynamic_slice_in_dim(w_sum[:, qc + kc + vc], here * own, own, 0)
    return (
        output,
        grad_tokens,
        gain1_grad,
        w_sum[:, :qc],
        w_sum[:, qc : qc + kc],
        w_sum[:, qc + kc : qc + kc + vc],
        wo_sum[:, :oc],
        gain2_grad,
        grad_gate[None],
        grad_up[None],
        grad_down[None],
    )


def solution(mesh):
    in_specs = (
        P(("dp", "tensor"), None),
        P(("dp", "tensor"), None),
        P("dp"),
        P("dp", "tensor"),
        P("dp", "tensor"),
        P("dp", "tensor"),
        P("dp", "tensor"),
        P("dp"),
        P("dp", None, "tensor"),
        P("dp", None, "tensor"),
        P("dp", "tensor", None),
        P("dp", None),
        P("dp", None),
        P("dp"),
    )
    out_specs = (
        P(("dp", "tensor"), None),
        P(("dp", "tensor"), None),
        P(("dp", "tensor")),
        P("dp", "tensor"),
        P("dp", "tensor"),
        P("dp", "tensor"),
        P("dp", "tensor"),
        P(("dp", "tensor")),
        P("dp", None, "tensor"),
        P("dp", None, "tensor"),
        P("dp", "tensor", None),
    )
    return jax.shard_map(
        on_device, mesh=mesh, in_specs=in_specs, out_specs=out_specs, check_vma=False
    )
```

```python
import functools

import jax
import jax.numpy as jnp
from jax import lax
from jax.experimental import pallas as pl
from jax.experimental.pallas import tpu as pltpu
from jax.sharding import PartitionSpec as P

HD = 64
DOCS = 3
EPS = 1e-06
THETA = 10000.0
BF = jnp.bfloat16
F32 = jnp.float32


def dot(a, b, dims):
    return lax.dot_general(a, b, (dims, ((), ())), preferred_element_type=F32)


def swap(x, mask):
    count = lax.axis_size("dp") * lax.axis_size("tensor")
    return lax.ppermute(x, ("dp", "tensor"), [(i, i ^ mask) for i in range(count)])


def gather_column(x, masks):
    blocks = [x] + [swap(x, mask) for mask in masks[1:]]
    return blocks + [swap(block, 1) for block in blocks]


def scatter_column(even, odd, masks):
    even = even.reshape((len(masks), -1) + even.shape[1:])
    got = swap(odd, 1).reshape(even.shape)
    total = even[0].astype(F32) + got[0].astype(F32)
    for n, mask in enumerate(masks):
        if mask:
            sent = (even[n].astype(F32) + got[n].astype(F32)).astype(BF)
            total = total + swap(sent, mask).astype(F32)
    return total


def exchange(x):
    half = lax.axis_size("dp") // 2
    planes = [[2 * i + z for i in range(half)] for z in range(2)]
    return lax.all_to_all(
        x, "dp", split_axis=0, concat_axis=0, tiled=True, axis_index_groups=planes
    )


def scatter_dp(parts, upper, columns):
    sums = jnp.sum(parts.astype(F32), axis=0)
    rows = sums.shape[0] // 2

    def keep(array):
        return jnp.where(upper, array[rows:], array[:rows])

    def send(array):
        return jnp.where(upper, array[:rows], array[rows:])

    gains = sums[:, columns:]
    gains = gains + swap(gains, 1) + swap(gains, 2) + swap(gains, 3)
    sums = sums[:, :columns]
    return (
        keep(sums) + swap(send(sums).astype(BF), 4).astype(F32),
        keep(gains) + swap(send(gains), 4),
    )


def rms_forward(rows):
    inverse = lax.rsqrt(jnp.mean(rows * rows, axis=1, keepdims=True) + EPS)
    return (rows * inverse, inverse)


def doc_positions(segment, index):
    onehot = (segment[:, None] == jnp.arange(DOCS, dtype=jnp.int32)[None, :]).astype(jnp.int32)
    counts = jnp.sum(onehot, axis=0)
    starts = jnp.cumsum(counts) - counts
    first = jnp.sum(onehot * starts[None, :], axis=1)
    return index - first


VMEM = 60 * 1024 * 1024


CHEAP = pl.CostEstimate(flops=10**9, bytes_accessed=2**20, transcendentals=0)
COST = pl.CostEstimate(flops=4 * 10**10, bytes_accessed=2**24, transcendentals=2**20)


def call(kernel, out_shape, scratch, name, *args):
    return pl.pallas_call(
        kernel,
        out_shape=out_shape,
        scratch_shapes=scratch,
        compiler_params=pltpu.CompilerParams(vmem_limit_bytes=VMEM),
        cost_estimate=COST,
        name=name,
    )(*args)


def shard_kernel(wq, wk, wv, wo, gain1, gain2, out):
    at = 0
    for ref in (wq, wk, wv, wo):
        out[:, at : at + ref.shape[1]] = ref[...]
        at += ref.shape[1]
    row = lax.broadcasted_iota(jnp.int32, (128, gain1.shape[1]), 0)
    gains = jnp.where(
        row == 0, gain1[...].astype(F32), jnp.where(row == 1, gain2[...].astype(F32), 0.0)
    )
    out[:, at:] = jnp.transpose(gains).astype(BF)


def spread_kernel(parity, shard, other, out):
    rows = shard.shape[0]
    upper = parity[0] == 1
    first = jnp.where(upper, other[...], shard[...])
    second = jnp.where(upper, shard[...], other[...])
    for n in range(out.shape[0]):
        out[n, :rows, :] = first
        out[n, rows:, :] = second


def pack_kernel(scaled, *refs):
    place = refs[0]
    blocks = refs[1:9]
    out, rows = refs[-2:]
    local = blocks[0].shape[0]

    @pl.when(pl.program_id(0) == 0)
    def _():
        for n, ref in enumerate(blocks):
            rows[n * local : (n + 1) * local, :] = ref[...]

    part = jnp.dot(place[...], rows[...], preferred_element_type=F32)
    if scaled:
        part = part * refs[9][...]
    out[...] = part.astype(BF)


def pack(place, blocks, gate):
    slots, count = place.shape
    local, width = blocks[0].shape
    tile = slots // 2
    gates = [] if gate is None else [gate]
    return pl.pallas_call(
        functools.partial(pack_kernel, gate is not None),
        grid=(slots // tile,),
        in_specs=[pl.BlockSpec((tile, count), lambda i: (i, 0))]
        + [pl.BlockSpec((local, width), lambda i: (0, 0))] * len(blocks)
        + [pl.BlockSpec((tile, 1), lambda i: (i, 0))] * len(gates),
        out_specs=pl.BlockSpec((tile, width), lambda i: (i, 0)),
        out_shape=jax.ShapeDtypeStruct((slots, width), BF),
        scratch_shapes=[pltpu.VMEM((count, width), BF)],
        compiler_params=pltpu.CompilerParams(vmem_limit_bytes=VMEM),
        cost_estimate=CHEAP,
        name="pack",
    )(place, *blocks, *gates)


def combine_kernel(scaled, *refs):
    place, slots = refs[:2]
    odd, even = refs[2 + scaled : 4 + scaled]
    step = pl.program_id(0)
    source = slots
    if scaled:
        source = refs[-1]

        @pl.when(step == 0)
        def _():
            source[...] = (slots[...].astype(F32) * refs[2][...]).astype(BF)

    part = dot(place[...], source[...], ((0,), (0,))).astype(BF)

    @pl.when(step == 0)
    def _():
        odd[...] = part

    @pl.when(step == 1)
    def _():
        even[...] = part


def combine(place, slots, gate):
    rows, count = place.shape
    width = slots.shape[1]
    tile = count // 2
    half = jax.ShapeDtypeStruct((count // 2, width), BF)
    scaled = gate is not None
    return pl.pallas_call(
        functools.partial(combine_kernel, int(scaled)),
        grid=(2,),
        in_specs=[
            pl.BlockSpec((rows, tile), lambda i: (0, 1 - i)),
            pl.BlockSpec((rows, width), lambda i: (0, 0)),
        ]
        + [pl.BlockSpec((rows, 1), lambda i: (0, 0))] * int(scaled),
        out_specs=[
            pl.BlockSpec((tile, width), lambda i: (0, 0)),
            pl.BlockSpec((tile, width), lambda i: (0, 0)),
        ],
        out_shape=(half, half),
        scratch_shapes=[pltpu.VMEM(slots.shape, BF)] if scaled else [],
        compiler_params=pltpu.CompilerParams(vmem_limit_bytes=VMEM),
        cost_estimate=COST,
        name="combine",
    )(place, slots, *([gate] if scaled else []))


def expert_rest_kernel(count, *refs):
    x, dy, hidden, dgate, dup = refs[:5]
    downs = refs[5 : 5 + count]
    produced, odd, even, wd = refs[5 + count :]
    units = downs[0].shape[0]
    for n in range(count):
        wd[n * units : (n + 1) * units, :] = downs[n][...]
    tile = 256
    for m in range(0, x.shape[0], tile):
        at = slice(m, m + tile)
        produced[at, :] = jnp.dot(
            hidden[at, :], wd[...], preferred_element_type=F32
        ).astype(BF)
    mid = odd.shape[1]
    for n, (left, right) in enumerate(((dgate, x), (dup, x), (hidden, dy))):
        odd[n, :, :] = dot(left[:, mid:], right[...], ((0,), (0,))).astype(BF)
        even[n, :, :] = dot(left[:, :mid], right[...], ((0,), (0,))).astype(BF)


def expert_rest(x, dy, hidden, dgate, dup, wd):
    rows, width = x.shape
    wide = hidden.shape[1]
    half = jax.ShapeDtypeStruct((3, wide // 2, width), BF)
    return call(
        functools.partial(expert_rest_kernel, len(wd)),
        (jax.ShapeDtypeStruct((rows, width), BF), half, half),
        [pltpu.VMEM((wide, width), BF)],
        "expert_rest",
        x,
        dy,
        hidden,
        dgate,
        dup,
        *wd,
    )


def turn(x, cosine, sine):
    lane = lax.broadcasted_iota(jnp.int32, x.shape, 1)
    half = HD // 2
    other = jnp.where(
        lane % HD < half, pltpu.roll(x, 2 * HD - half, 1), pltpu.roll(x, half, 1)
    )
    return x * cosine + other * sine


def attention_kernel(heads, ratio, *refs):
    (t0, t1, t2, t3, full, cosine, sine, mask) = refs[:8]
    (odd_out, even_out, normed_out, qkv_out, attended_out, probs_out) = refs[8:]
    qc = heads * HD
    kc = qc // ratio
    qkvc = qc + 2 * kc
    width = full.shape[0]
    local = t0.shape[0]
    group = 4 * local
    gains = jnp.transpose(full[:, qkvc + qc :].astype(F32))
    gain1 = gains[0:1, :]
    for n, ref in enumerate((t0, t1, t2, t3)):
        rows = ref[...].astype(F32)
        inverse = lax.rsqrt(jnp.mean(rows * rows, axis=1, keepdims=True) + EPS)
        normed_out[n * local : (n + 1) * local, :] = (rows * inverse * gain1).astype(BF)
    for n in range(4):
        at = slice(n * local, (n + 1) * local)
        projected = jnp.dot(normed_out[at, :], full[:, :qkvc], preferred_element_type=F32)
        for c in range(0, qc + kc, 2 * HD):
            turned = turn(projected[:, c : c + 2 * HD], cosine[at, :], sine[at, :])
            qkv_out[at, c : c + 2 * HD] = turned.astype(BF)
        qkv_out[at, qc + kc :] = projected[:, qc + kc :].astype(BF)
    scale = HD ** (-0.5)
    values_t = jnp.transpose(qkv_out[:, qc + kc :])
    wide = local * 2
    for j in range(0, group, wide):
        outs = []
        for h in range(heads):
            kv = h // ratio
            keys = qkv_out[:, qc + kv * HD : qc + (kv + 1) * HD]
            queries = qkv_out[j : j + wide, h * HD : (h + 1) * HD]
            scores = dot(keys, queries, ((1,), (1,))) * scale + mask[:, j : j + wide]
            weights = jnp.exp(scores - jnp.max(scores, axis=0, keepdims=True))
            total = jnp.sum(weights, axis=0, keepdims=True)
            probs = (weights * (1.0 / total)).astype(BF)
            probs_out[h, :, j : j + wide] = probs
            outs.append(
                jnp.dot(
                    values_t[kv * HD : (kv + 1) * HD], probs, preferred_element_type=F32
                )
            )
        attended = jnp.transpose(jnp.concatenate(outs, axis=0)).astype(BF)
        attended_out[j : j + wide, :] = attended
        partial = dot(attended, full[:, qkvc : qkvc + qc], ((1,), (1,))).astype(BF)
        if j == 0:
            even_out[...] = partial
        else:
            odd_out[...] = partial


def attention(blocks, full, cosine, sine, mask, heads, ratio):
    local, width = blocks[0].shape
    group = 4 * local
    qc = heads * HD
    qkvc = qc + 2 * (qc // ratio)
    shape = jax.ShapeDtypeStruct
    return pl.pallas_call(
        functools.partial(attention_kernel, heads, ratio),
        out_shape=(
            shape((group // 2, width), BF),
            shape((group // 2, width), BF),
            shape((group, width), BF),
            shape((group, qkvc), BF),
            shape((group, qc), BF),
            shape((heads, group, group), BF),
        ),
        compiler_params=pltpu.CompilerParams(vmem_limit_bytes=VMEM),
        cost_estimate=COST,
        name="attention_forward",
    )(*blocks, full, cosine, sine, mask)


def attention_back_kernel(heads, ratio, *refs):
    (b0, b1, b2, b3, full, cosine, sine, normed, qkv, attended, probs, gain2) = refs[:12]
    (odd_out, even_out, grads_out) = refs[12:15]
    (gatt, dqkv, branch) = refs[15:]
    qc = heads * HD
    kc = qc // ratio
    qkvc = qc + 2 * kc
    width = full.shape[0]
    local = b0.shape[0]
    group = 4 * local
    scale = HD ** (-0.5)
    for n, ref in enumerate((b0, b1, b2, b3)):
        at = slice(n * local, (n + 1) * local)
        branch[at, :] = ref[...]
        gatt[at, :] = jnp.dot(
            ref[...], full[:, qkvc : qkvc + qc], preferred_element_type=F32
        ).astype(BF)
    grads_out[:, qkvc : qkvc + qc] = dot(branch[...], attended[...], ((0,), (0,))).astype(BF)
    wide = local * 2
    keys_t = jnp.transpose(qkv[:, qc : qc + kc])
    grad_k = [None] * (heads // ratio)
    grad_v = [None] * (heads // ratio)
    for j in range(0, group, wide):
        outs = []
        for h in range(heads):
            kv = h // ratio
            values = qkv[:, qc + kc + kv * HD : qc + kc + (kv + 1) * HD]
            queries = qkv[j : j + wide, h * HD : (h + 1) * HD]
            grad_out = gatt[j : j + wide, h * HD : (h + 1) * HD]
            low = probs[h, :, j : j + wide]
            grad_probs = dot(values, grad_out, ((1,), (1,)))
            prob = low.astype(F32)
            weighted = prob * grad_probs
            inner = jnp.sum(weighted, axis=0, keepdims=True)
            grad_scores = (weighted - prob * inner).astype(BF)
            gk = jnp.dot(grad_scores, queries, preferred_element_type=F32)
            gv = jnp.dot(low, grad_out, preferred_element_type=F32)
            grad_k[kv] = gk if grad_k[kv] is None else grad_k[kv] + gk
            grad_v[kv] = gv if grad_v[kv] is None else grad_v[kv] + gv
            outs.append(
                jnp.dot(
                    keys_t[kv * HD : (kv + 1) * HD], grad_scores, preferred_element_type=F32
                )
            )
        grad_q = jnp.transpose(jnp.concatenate(outs, axis=0)) * scale
        for c in range(0, qc, 2 * HD):
            turned = turn(grad_q[:, c : c + 2 * HD], cosine[j : j + wide, :], -sine[j : j + wide, :])
            dqkv[j : j + wide, c : c + 2 * HD] = turned.astype(BF)
    grad_k = jnp.concatenate(grad_k, axis=1) * scale
    for c in range(0, kc, 2 * HD):
        turned = turn(grad_k[:, c : c + 2 * HD], cosine[...], -sine[...])
        dqkv[:, qc + c : qc + c + 2 * HD] = turned.astype(BF)
    dqkv[:, qc + kc :] = jnp.concatenate(grad_v, axis=1).astype(BF)
    grads_out[:, :qkvc] = dot(normed[...], dqkv[...], ((0,), (0,))).astype(BF)
    gain1_sum = jnp.zeros((1, width), F32)
    for n in range(4):
        at = slice(n * local, (n + 1) * local)
        grad_normed = dot(dqkv[at, :], full[:, :qkvc], ((1,), (1,)))
        gain1_sum = gain1_sum + jnp.sum(
            grad_normed * normed[at, :].astype(F32), axis=0, keepdims=True
        )
        out = even_out if n < 2 else odd_out
        out[(n % 2) * local : (n % 2 + 1) * local, :] = grad_normed.astype(BF)
    gains = jnp.transpose(full[:, qkvc + qc :].astype(F32))
    row = lax.broadcasted_iota(jnp.int32, (128, width), 0)
    sums = jnp.where(row == 0, gain1_sum / gains[0:1, :], jnp.where(row == 1, gain2[...], 0.0))
    grads_out[:, qkvc + qc :] = jnp.transpose(sums).astype(BF)


def attention_back(blocks, full, cosine, sine, normed, qkv, attended, probs, gain2, heads, ratio):
    local, width = blocks[0].shape
    group = 4 * local
    qc = heads * HD
    shape = jax.ShapeDtypeStruct
    return pl.pallas_call(
        functools.partial(attention_back_kernel, heads, ratio),
        out_shape=(
            shape((group // 2, width), BF),
            shape((group // 2, width), BF),
            shape(full.shape, BF),
        ),
        scratch_shapes=[
            pltpu.VMEM((group, qc), BF),
            pltpu.VMEM((group, qkv.shape[1]), BF),
            pltpu.VMEM((group, width), BF),
        ],
        compiler_params=pltpu.CompilerParams(vmem_limit_bytes=VMEM),
        cost_estimate=CHEAP,
        name="attention_backward",
    )(*blocks, full, cosine, sine, normed, qkv, attended, probs, gain2)


def expert_kernel(count, *refs):
    x, dy = refs[:2]
    weights = refs[2 : 2 + 3 * count]
    grad_in, hidden_out, dgate_out, dup_out, wg, wu, wd = refs[2 + 3 * count :]
    units = weights[0].shape[1]

    @pl.when(pl.program_id(0) == 0)
    def _():
        for n in range(count):
            at = slice(n * units, (n + 1) * units)
            wg[:, at] = weights[n][...]
            wu[:, at] = weights[count + n][...]
            wd[at, :] = weights[2 * count + n][...]

    gate = jnp.dot(x[...], wg[...], preferred_element_type=F32)
    up = jnp.dot(x[...], wu[...], preferred_element_type=F32)
    sigma = jax.nn.sigmoid(gate)
    silu = gate * sigma
    hidden_out[...] = (silu * up).astype(BF)
    grad_hidden = dot(dy[...], wd[...], ((1,), (1,)))
    dgate = (grad_hidden * up * sigma * (1.0 + gate * (1.0 - sigma))).astype(BF)
    dup = (grad_hidden * silu).astype(BF)
    dgate_out[...] = dgate
    dup_out[...] = dup
    grad_in[...] = (
        dot(dgate, wg[...], ((1,), (1,))) + dot(dup, wu[...], ((1,), (1,)))
    ).astype(BF)


def expert_layer(x, dy, wg, wu, wd):
    rows, width = x.shape
    units = wg[0].shape[1]
    count = len(wg)
    wide = count * units
    tile = rows // 2
    shape = jax.ShapeDtypeStruct

    def tiled(columns):
        return pl.BlockSpec((tile, columns), lambda i: (i, 0))

    def whole(array):
        return pl.BlockSpec(array.shape, lambda i: (0, 0))

    weights = list(wg) + list(wu) + list(wd)
    return pl.pallas_call(
        functools.partial(expert_kernel, count),
        grid=(rows // tile,),
        in_specs=[tiled(width), tiled(width)] + [whole(w) for w in weights],
        out_specs=[tiled(width), tiled(wide), tiled(wide), tiled(wide)],
        out_shape=(
            shape((rows, width), BF),
            shape((rows, wide), BF),
            shape((rows, wide), BF),
            shape((rows, wide), BF),
        ),
        scratch_shapes=[
            pltpu.VMEM((width, wide), BF),
            pltpu.VMEM((width, wide), BF),
            pltpu.VMEM((wide, width), BF),
        ],
        compiler_params=pltpu.CompilerParams(vmem_limit_bytes=VMEM),
        cost_estimate=COST,
        name="expert_layer",
    )(x, dy, *weights)


def on_device(
    tokens,
    cotangent,
    norm1_gain,
    w_query,
    w_key,
    w_value,
    w_out,
    norm2_gain,
    expert_gate,
    expert_up,
    expert_down,
    route_gates,
    routes,
    segment,
):
    group = segment.shape[0]
    local, width = tokens.shape
    top_k = routes.shape[1]
    dp_count = lax.axis_size("dp")
    tensor_count = lax.axis_size("tensor")
    experts = expert_gate.shape[0] * dp_count
    capacity = min(group, group * top_k * 5 // (4 * experts))
    share = capacity // tensor_count
    half = dp_count // 2
    slots = half * 2 * share
    four = [0, 2]
    eight = [0, 2, 4, 6]
    parity = lax.axis_index("dp") % 2
    upper = parity == 1
    piece = width // dp_count
    here = lax.axis_index("tensor")
    qc, kc, vc, oc = w_query.shape[1], w_key.shape[1], w_value.shape[1], w_out.shape[1]
    heads = qc // HD
    ratio = qc // kc

    qkvc = qc + kc + vc
    full_shape = (2 * w_query.shape[0], qkvc + oc + 128)
    shard = call(
        shard_kernel,
        jax.ShapeDtypeStruct((w_query.shape[0], full_shape[1]), BF),
        [],
        "weight_shard",
        w_query,
        w_key,
        w_value,
        w_out,
        norm1_gain.reshape(1, -1),
        norm2_gain.reshape(1, -1),
    )
    other = swap(shard, 4)
    spread = pl.pallas_call(
        spread_kernel,
        in_specs=[
            pl.BlockSpec(memory_space=pltpu.SMEM),
            pl.BlockSpec(memory_space=pltpu.VMEM),
            pl.BlockSpec(memory_space=pltpu.VMEM),
        ],
        out_shape=jax.ShapeDtypeStruct((half,) + full_shape, BF),
        compiler_params=pltpu.CompilerParams(vmem_limit_bytes=VMEM),
        name="weight_spread",
    )(parity.reshape(1).astype(jnp.int32), shard, other)
    spread, tok, cot, routes, route_gates, segment = lax.optimization_barrier(
        (spread, tokens, cotangent, routes, route_gates, segment)
    )
    full = exchange(spread).reshape(half * full_shape[0], full_shape[1])
    token_blocks = gather_column(tok, four)
    cot_far = [cot] + [swap(cot, mask) for mask in eight[1:]]
    cot_far, own_weights = lax.optimization_barrier(
        (cot_far, [expert_gate[0], expert_up[0], expert_down[0]])
    )
    cot_blocks = cot_far + [swap(block, 1) for block in cot_far]
    far_weights = [swap(w, 2) for w in own_weights]

    order = jnp.array([0, 2, 1, 3], jnp.int32) ^ here
    index = (order[:, None] * local + jnp.arange(local, dtype=jnp.int32)[None, :]).reshape(group)

    def reorder(x):
        split = x.reshape((tensor_count, local) + x.shape[1:])
        return jnp.concatenate(
            [lax.dynamic_index_in_dim(split, here ^ s, 0, False) for s in (0, 2, 1, 3)]
        )

    def pair_up(own, other):
        mid = own.shape[0] // 2
        return jnp.concatenate([own[:mid], other[:mid], own[mid:], other[mid:]])

    seg = reorder(segment)
    route_rows = pair_up(reorder(routes), reorder(swap(routes, 4)))
    gate_rows = pair_up(reorder(route_gates), reorder(swap(route_gates, 4)))
    pair_index = pair_up(index, index)
    pair_group = pair_up(jnp.zeros_like(index), jnp.ones_like(index))

    expert_ids = 2 * jnp.arange(half, dtype=jnp.int32) + parity
    hit = route_rows[None, :, :] == expert_ids[:, None, None]
    mine = pair_group[None, :] == jnp.arange(2, dtype=jnp.int32)[:, None]
    member = (jnp.any(hit, axis=2)[:, None, :] & mine[None]).reshape(2 * half, 2 * group)
    gate_of = jnp.sum(jnp.where(hit, gate_rows[None], 0.0), axis=2)
    gate_of = jnp.broadcast_to(gate_of[:, None, :], (half, 2, 2 * group)).reshape(member.shape)
    before = (pair_index[:, None] < pair_index[None, :]).astype(BF)
    slot = dot(member.astype(BF), before, ((1,), (0,)))
    slot = jnp.where(member, slot, -1.0).astype(jnp.int32)
    wanted = here * share + jnp.arange(share, dtype=jnp.int32)
    place = slot[:, None, :] == wanted[None, :, None]
    slot_gate = jnp.sum(jnp.where(place, gate_of[:, None, :], 0.0), axis=2).reshape(slots)
    place = place.astype(BF).reshape(slots, 2 * group)

    slot_gate = slot_gate.reshape(slots, 1)
    places = doc_positions(seg, index).astype(F32)
    freqs = THETA ** (-(jnp.arange(HD // 2, dtype=F32) * 2.0) / HD)
    angle = places[:, None] * freqs[None, :]
    cosine, sine = jnp.cos(angle), jnp.sin(angle)
    cosine = jnp.concatenate([cosine] * 4, axis=1)
    sine = jnp.concatenate([-sine, sine, -sine, sine], axis=1)
    allowed = (seg[:, None] == seg[None, :]) & (index[:, None] <= index[None, :])
    mask = jnp.where(allowed, 0.0, -1e30).astype(F32)
    grad_packed = pack(place, cot_blocks, slot_gate)
    full, grad_packed = lax.optimization_barrier((full, grad_packed))
    grad_arrived = exchange(grad_packed)
    odd, even, normed1, qkv, attended, probs = attention(
        token_blocks, full, cosine, sine, mask, heads, ratio
    )
    gain1 = full[:, qkvc + oc].astype(F32)
    gain2 = full[:, qkvc + oc + 1].astype(F32)
    odd, even, own_weights, far_weights = lax.optimization_barrier(
        (odd, even, own_weights, far_weights)
    )
    near_weights = [swap(w, 1) for w in own_weights]
    last_weights = [swap(w, 1) for w in far_weights]
    wg, wu, wd = zip(own_weights, far_weights, near_weights, last_weights)
    mixed = tokens.astype(F32) + scatter_column(even, odd, four)

    normal2, inverse2 = rms_forward(mixed)
    normed2 = (normal2 * gain2[None, :]).astype(BF)
    arrived = exchange(pack(place, gather_column(normed2, eight), None))

    grad_inputs, hidden, grad_gate_pre, grad_up_pre = expert_layer(
        arrived, grad_arrived, wg, wu, wd
    )
    grad_back = exchange(grad_inputs)
    produced, units_odd, units_even = expert_rest(
        arrived, grad_arrived, hidden, grad_gate_pre, grad_up_pre, wd
    )
    units_got = swap(units_odd, 1)
    count = units_even.shape[1] // 2
    units_mine = units_even[:, :count].astype(F32) + units_got[:, :count].astype(F32)
    units_sent = (
        units_even[:, count:].astype(F32) + units_got[:, count:].astype(F32)
    ).astype(BF)
    grad_back, produced, units_mine, units_sent = lax.optimization_barrier(
        (grad_back, produced, units_mine, units_sent)
    )
    returned = exchange(produced)

    odd, even = combine(place, grad_back, None)
    grad_normed2 = scatter_column(even, odd, eight)
    scaled = grad_normed2 * gain2[None, :]
    inner = jnp.mean(scaled * normal2, axis=1, keepdims=True)
    grad_mixed = cotangent.astype(F32) + inverse2 * (scaled - normal2 * inner)
    gain2_part = jnp.sum(grad_normed2 * normal2, axis=0, keepdims=True)
    grad_branch = gather_column(grad_mixed.astype(BF), four)

    grad_branch, units_sent = lax.optimization_barrier((grad_branch, units_sent))
    units_far = swap(units_sent, 2)

    odd, even, grads = attention_back(
        grad_branch, full, cosine, sine, normed1, qkv, attended, probs, gain2_part, heads, ratio
    )
    odd, even, returned = lax.optimization_barrier((odd, even, returned))
    grad_units = units_mine + units_far.astype(F32)
    grad_gate, grad_up, grad_down = grad_units[0].T, grad_units[1].T, grad_units[2]
    parts = exchange(grads.reshape(half, width // half, grads.shape[1]))
    grad_normed1 = scatter_column(even, odd, four)
    normal1, inverse1 = rms_forward(tokens.astype(F32))
    scaled = grad_normed1 * gain1[None, :]
    inner = jnp.mean(scaled * normal1, axis=1, keepdims=True)
    grad_tokens = grad_mixed + inverse1 * (scaled - normal1 * inner)

    odd, even = combine(place, returned, slot_gate)
    output = mixed + scatter_column(even, odd, eight)
    parts, output, grad_tokens, grad_gate, grad_up, grad_down = lax.optimization_barrier(
        (parts, output, grad_tokens, grad_gate, grad_up, grad_down)
    )
    w_sum, gain_sums = scatter_dp(parts, upper, qkvc + oc)
    own = piece // tensor_count
    gain1_grad = lax.dynamic_slice_in_dim(gain_sums[:, 0], here * own, own, 0)
    gain2_grad = lax.dynamic_slice_in_dim(gain_sums[:, 1], here * own, own, 0)
    return (
        output,
        grad_tokens,
        gain1_grad,
        w_sum[:, :qc],
        w_sum[:, qc : qc + kc],
        w_sum[:, qc + kc : qc + kc + vc],
        w_sum[:, qkvc : qkvc + oc],
        gain2_grad,
        grad_gate[None],
        grad_up[None],
        grad_down[None],
    )


def solution(mesh):
    in_specs = (
        P(("dp", "tensor"), None),
        P(("dp", "tensor"), None),
        P("dp"),
        P("dp", "tensor"),
        P("dp", "tensor"),
        P("dp", "tensor"),
        P("dp", "tensor"),
        P("dp"),
        P("dp", None, "tensor"),
        P("dp", None, "tensor"),
        P("dp", "tensor", None),
        P("dp", None),
        P("dp", None),
        P("dp"),
    )
    out_specs = (
        P(("dp", "tensor"), None),
        P(("dp", "tensor"), None),
        P(("dp", "tensor")),
        P("dp", "tensor"),
        P("dp", "tensor"),
        P("dp", "tensor"),
        P("dp", "tensor"),
        P(("dp", "tensor")),
        P("dp", None, "tensor"),
        P("dp", None, "tensor"),
        P("dp", "tensor", None),
    )
    return jax.shard_map(
        on_device, mesh=mesh, in_specs=in_specs, out_specs=out_specs, check_vma=False
    )
```

```python
import functools

import jax
import jax.numpy as jnp
from jax import lax
from jax.experimental import pallas as pl
from jax.experimental.pallas import tpu as pltpu
from jax.sharding import PartitionSpec as P

HD = 64
DOCS = 3
EPS = 1e-06
THETA = 10000.0
BF = jnp.bfloat16
F32 = jnp.float32


def dot(a, b, dims):
    return lax.dot_general(a, b, (dims, ((), ())), preferred_element_type=F32)


def swap(x, mask):
    count = lax.axis_size("dp") * lax.axis_size("tensor")
    return lax.ppermute(x, ("dp", "tensor"), [(i, i ^ mask) for i in range(count)])


def gather_column(x, masks):
    blocks = [x] + [swap(x, mask) for mask in masks[1:]]
    return blocks + [swap(block, 1) for block in blocks]


def scatter_column(even, odd, masks):
    total, sent = scatter_near(even, odd, masks)
    return scatter_far(total, sent, masks)


def scatter_near(even, odd, masks):
    even = even.reshape((len(masks), -1) + even.shape[1:])
    got = swap(odd, 1).reshape(even.shape)
    sums = [even[n].astype(F32) + got[n].astype(F32) for n in range(len(masks))]
    return sums[0], [part.astype(BF) for part in sums[1:]]


def scatter_far(total, sent, masks):
    for mask, part in zip(masks[1:], sent):
        total = total + swap(part, mask).astype(F32)
    return total


def exchange(x):
    half = lax.axis_size("dp") // 2
    planes = [[2 * i + z for i in range(half)] for z in range(2)]
    return lax.all_to_all(
        x, "dp", split_axis=0, concat_axis=0, tiled=True, axis_index_groups=planes
    )


def scatter_dp(parts, upper, columns):
    sums = jnp.sum(parts.astype(F32), axis=0)
    rows = sums.shape[0] // 2

    def keep(array):
        return jnp.where(upper, array[rows:], array[:rows])

    def send(array):
        return jnp.where(upper, array[:rows], array[rows:])

    gains = sums[:, columns:]
    gains = gains + swap(gains, 1) + swap(gains, 2) + swap(gains, 3)
    sums = sums[:, :columns]
    return (
        keep(sums) + swap(send(sums).astype(BF), 4).astype(F32),
        keep(gains) + swap(send(gains), 4),
    )


def rms_forward(rows):
    inverse = lax.rsqrt(jnp.mean(rows * rows, axis=1, keepdims=True) + EPS)
    return (rows * inverse, inverse)


def doc_positions(segment, index):
    onehot = (segment[:, None] == jnp.arange(DOCS, dtype=jnp.int32)[None, :]).astype(jnp.int32)
    counts = jnp.sum(onehot, axis=0)
    starts = jnp.cumsum(counts) - counts
    first = jnp.sum(onehot * starts[None, :], axis=1)
    return index - first


VMEM = 63 * 1024 * 1024


CHEAP = pl.CostEstimate(flops=10**9, bytes_accessed=2**20, transcendentals=0)
COST = pl.CostEstimate(flops=4 * 10**10, bytes_accessed=2**24, transcendentals=2**20)


def call(kernel, out_shape, scratch, name, *args):
    return pl.pallas_call(
        kernel,
        out_shape=out_shape,
        scratch_shapes=scratch,
        compiler_params=pltpu.CompilerParams(vmem_limit_bytes=VMEM),
        cost_estimate=COST,
        name=name,
    )(*args)


def shard_kernel(wq, wk, wv, wo, gain1, gain2, out):
    at = 0
    for ref in (wq, wk, wv, wo):
        out[:, at : at + ref.shape[1]] = ref[...]
        at += ref.shape[1]
    row = lax.broadcasted_iota(jnp.int32, (128, gain1.shape[1]), 0)
    gains = jnp.where(
        row == 0, gain1[...].astype(F32), jnp.where(row == 1, gain2[...].astype(F32), 0.0)
    )
    out[:, at:] = jnp.transpose(gains).astype(BF)


def spread_kernel(parity, shard, other, out):
    rows = shard.shape[0]
    upper = parity[0] == 1
    first = jnp.where(upper, other[...], shard[...])
    second = jnp.where(upper, shard[...], other[...])
    for n in range(out.shape[0]):
        out[n, :rows, :] = first
        out[n, rows:, :] = second


def pack_kernel(scaled, *refs):
    place = refs[0]
    blocks = refs[1:9]
    out, rows = refs[-2:]
    local = blocks[0].shape[0]

    @pl.when(pl.program_id(0) == 0)
    def _():
        for n, ref in enumerate(blocks):
            rows[n * local : (n + 1) * local, :] = ref[...]

    part = jnp.dot(place[...], rows[...], preferred_element_type=F32)
    if scaled:
        part = part * refs[9][...]
    out[...] = part.astype(BF)


def pack(place, blocks, gate):
    slots, count = place.shape
    local, width = blocks[0].shape
    tile = slots // 2
    gates = [] if gate is None else [gate]
    return pl.pallas_call(
        functools.partial(pack_kernel, gate is not None),
        grid=(slots // tile,),
        in_specs=[pl.BlockSpec((tile, count), lambda i: (i, 0))]
        + [pl.BlockSpec((local, width), lambda i: (0, 0))] * len(blocks)
        + [pl.BlockSpec((tile, 1), lambda i: (i, 0))] * len(gates),
        out_specs=pl.BlockSpec((tile, width), lambda i: (i, 0)),
        out_shape=jax.ShapeDtypeStruct((slots, width), BF),
        scratch_shapes=[pltpu.VMEM((count, width), BF)],
        compiler_params=pltpu.CompilerParams(vmem_limit_bytes=VMEM),
        cost_estimate=CHEAP,
        name="pack",
    )(place, *blocks, *gates)


def combine_kernel(scaled, *refs):
    place, slots = refs[:2]
    odd, even = refs[2 + scaled : 4 + scaled]
    step = pl.program_id(0)
    source = slots
    if scaled:
        source = refs[-1]

        @pl.when(step == 0)
        def _():
            source[...] = (slots[...].astype(F32) * refs[2][...]).astype(BF)

    part = dot(place[...], source[...], ((0,), (0,))).astype(BF)

    @pl.when(step == 0)
    def _():
        odd[...] = part

    @pl.when(step == 1)
    def _():
        even[...] = part


def combine(place, slots, gate):
    rows, count = place.shape
    width = slots.shape[1]
    tile = count // 2
    half = jax.ShapeDtypeStruct((count // 2, width), BF)
    scaled = gate is not None
    return pl.pallas_call(
        functools.partial(combine_kernel, int(scaled)),
        grid=(2,),
        in_specs=[
            pl.BlockSpec((rows, tile), lambda i: (0, 1 - i)),
            pl.BlockSpec((rows, width), lambda i: (0, 0)),
        ]
        + [pl.BlockSpec((rows, 1), lambda i: (0, 0))] * int(scaled),
        out_specs=[
            pl.BlockSpec((tile, width), lambda i: (0, 0)),
            pl.BlockSpec((tile, width), lambda i: (0, 0)),
        ],
        out_shape=(half, half),
        scratch_shapes=[pltpu.VMEM(slots.shape, BF)] if scaled else [],
        compiler_params=pltpu.CompilerParams(vmem_limit_bytes=VMEM),
        cost_estimate=COST,
        name="combine",
    )(place, slots, *([gate] if scaled else []))


def expert_rest_kernel(count, *refs):
    x, dy, hidden, dgate, dup = refs[:5]
    downs = refs[5 : 5 + count]
    produced, odd, even, wd = refs[5 + count :]
    units = downs[0].shape[0]
    for n in range(count):
        wd[n * units : (n + 1) * units, :] = downs[n][...]
    tile = 256
    for m in range(0, x.shape[0], tile):
        at = slice(m, m + tile)
        produced[at, :] = jnp.dot(
            hidden[at, :], wd[...], preferred_element_type=F32
        ).astype(BF)
    mid = odd.shape[1]
    for n, (left, right) in enumerate(((dgate, x), (dup, x), (hidden, dy))):
        odd[n, :, :] = dot(left[:, mid:], right[...], ((0,), (0,))).astype(BF)
        even[n, :, :] = dot(left[:, :mid], right[...], ((0,), (0,))).astype(BF)


def expert_rest(x, dy, hidden, dgate, dup, wd):
    rows, width = x.shape
    wide = hidden.shape[1]
    half = jax.ShapeDtypeStruct((3, wide // 2, width), BF)
    return call(
        functools.partial(expert_rest_kernel, len(wd)),
        (jax.ShapeDtypeStruct((rows, width), BF), half, half),
        [pltpu.VMEM((wide, width), BF)],
        "expert_rest",
        x,
        dy,
        hidden,
        dgate,
        dup,
        *wd,
    )


def turn(x, cosine, sine):
    lane = lax.broadcasted_iota(jnp.int32, x.shape, 1)
    half = HD // 2
    other = jnp.where(
        lane % HD < half, pltpu.roll(x, 2 * HD - half, 1), pltpu.roll(x, half, 1)
    )
    return x * cosine + other * sine


def attention_kernel(heads, ratio, *refs):
    (t0, t1, t2, t3, full, cosine, sine, mask) = refs[:8]
    (odd_out, even_out, normed_out, qkv_out, attended_out, probs_out) = refs[8:]
    qc = heads * HD
    kc = qc // ratio
    qkvc = qc + 2 * kc
    width = full.shape[0]
    local = t0.shape[0]
    group = 4 * local
    gains = jnp.transpose(full[:, qkvc + qc :].astype(F32))
    gain1 = gains[0:1, :]
    for n, ref in enumerate((t0, t1, t2, t3)):
        rows = ref[...].astype(F32)
        inverse = lax.rsqrt(jnp.mean(rows * rows, axis=1, keepdims=True) + EPS)
        normed_out[n * local : (n + 1) * local, :] = (rows * inverse * gain1).astype(BF)
    for n in range(4):
        at = slice(n * local, (n + 1) * local)
        projected = jnp.dot(normed_out[at, :], full[:, :qkvc], preferred_element_type=F32)
        for c in range(0, qc + kc, 2 * HD):
            turned = turn(projected[:, c : c + 2 * HD], cosine[at, :], sine[at, :])
            qkv_out[at, c : c + 2 * HD] = turned.astype(BF)
        qkv_out[at, qc + kc :] = projected[:, qc + kc :].astype(BF)
    scale = HD ** (-0.5)
    values_t = jnp.transpose(qkv_out[:, qc + kc :])
    wide = local * 2
    for j in range(0, group, wide):
        outs = []
        for h in range(heads):
            kv = h // ratio
            keys = qkv_out[:, qc + kv * HD : qc + (kv + 1) * HD]
            queries = qkv_out[j : j + wide, h * HD : (h + 1) * HD]
            scores = dot(keys, queries, ((1,), (1,))) * scale + mask[:, j : j + wide]
            weights = jnp.exp(scores - jnp.max(scores, axis=0, keepdims=True))
            total = jnp.sum(weights, axis=0, keepdims=True)
            probs = (weights * (1.0 / total)).astype(BF)
            probs_out[h, :, j : j + wide] = probs
            outs.append(
                jnp.dot(
                    values_t[kv * HD : (kv + 1) * HD], probs, preferred_element_type=F32
                )
            )
        attended = jnp.transpose(jnp.concatenate(outs, axis=0)).astype(BF)
        attended_out[j : j + wide, :] = attended
        partial = dot(attended, full[:, qkvc : qkvc + qc], ((1,), (1,))).astype(BF)
        if j == 0:
            even_out[...] = partial
        else:
            odd_out[...] = partial


def attention(blocks, full, cosine, sine, mask, heads, ratio):
    local, width = blocks[0].shape
    group = 4 * local
    qc = heads * HD
    qkvc = qc + 2 * (qc // ratio)
    shape = jax.ShapeDtypeStruct
    return pl.pallas_call(
        functools.partial(attention_kernel, heads, ratio),
        out_shape=(
            shape((group // 2, width), BF),
            shape((group // 2, width), BF),
            shape((group, width), BF),
            shape((group, qkvc), BF),
            shape((group, qc), BF),
            shape((heads, group, group), BF),
        ),
        compiler_params=pltpu.CompilerParams(vmem_limit_bytes=VMEM),
        cost_estimate=COST,
        name="attention_forward",
    )(*blocks, full, cosine, sine, mask)


def attention_back_kernel(heads, ratio, *refs):
    (b0, b1, b2, b3, full, cosine, sine, normed, qkv, attended, probs, gain2) = refs[:12]
    (odd_out, even_out, grads_out) = refs[12:15]
    (gatt, dqkv, branch) = refs[15:]
    qc = heads * HD
    kc = qc // ratio
    qkvc = qc + 2 * kc
    width = full.shape[0]
    local = b0.shape[0]
    group = 4 * local
    scale = HD ** (-0.5)
    for n, ref in enumerate((b0, b1, b2, b3)):
        at = slice(n * local, (n + 1) * local)
        branch[at, :] = ref[...]
        gatt[at, :] = jnp.dot(
            ref[...], full[:, qkvc : qkvc + qc], preferred_element_type=F32
        ).astype(BF)
    grads_out[:, qkvc : qkvc + qc] = dot(branch[...], attended[...], ((0,), (0,))).astype(BF)
    wide = local * 2
    keys_t = jnp.transpose(qkv[:, qc : qc + kc])
    grad_k = [None] * (heads // ratio)
    grad_v = [None] * (heads // ratio)
    for j in range(0, group, wide):
        outs = []
        for h in range(heads):
            kv = h // ratio
            values = qkv[:, qc + kc + kv * HD : qc + kc + (kv + 1) * HD]
            queries = qkv[j : j + wide, h * HD : (h + 1) * HD]
            grad_out = gatt[j : j + wide, h * HD : (h + 1) * HD]
            low = probs[h, :, j : j + wide]
            grad_probs = dot(values, grad_out, ((1,), (1,)))
            prob = low.astype(F32)
            weighted = prob * grad_probs
            inner = jnp.sum(weighted, axis=0, keepdims=True)
            grad_scores = (weighted - prob * inner).astype(BF)
            gk = jnp.dot(grad_scores, queries, preferred_element_type=F32)
            gv = jnp.dot(low, grad_out, preferred_element_type=F32)
            grad_k[kv] = gk if grad_k[kv] is None else grad_k[kv] + gk
            grad_v[kv] = gv if grad_v[kv] is None else grad_v[kv] + gv
            outs.append(
                jnp.dot(
                    keys_t[kv * HD : (kv + 1) * HD], grad_scores, preferred_element_type=F32
                )
            )
        grad_q = jnp.transpose(jnp.concatenate(outs, axis=0)) * scale
        for c in range(0, qc, 2 * HD):
            turned = turn(grad_q[:, c : c + 2 * HD], cosine[j : j + wide, :], -sine[j : j + wide, :])
            dqkv[j : j + wide, c : c + 2 * HD] = turned.astype(BF)
    grad_k = jnp.concatenate(grad_k, axis=1) * scale
    for c in range(0, kc, 2 * HD):
        turned = turn(grad_k[:, c : c + 2 * HD], cosine[...], -sine[...])
        dqkv[:, qc + c : qc + c + 2 * HD] = turned.astype(BF)
    dqkv[:, qc + kc :] = jnp.concatenate(grad_v, axis=1).astype(BF)
    grads_out[:, :qkvc] = dot(normed[...], dqkv[...], ((0,), (0,))).astype(BF)
    gain1_sum = jnp.zeros((1, width), F32)
    for n in range(4):
        at = slice(n * local, (n + 1) * local)
        grad_normed = dot(dqkv[at, :], full[:, :qkvc], ((1,), (1,)))
        gain1_sum = gain1_sum + jnp.sum(
            grad_normed * normed[at, :].astype(F32), axis=0, keepdims=True
        )
        out = even_out if n < 2 else odd_out
        out[(n % 2) * local : (n % 2 + 1) * local, :] = grad_normed.astype(BF)
    gains = jnp.transpose(full[:, qkvc + qc :].astype(F32))
    row = lax.broadcasted_iota(jnp.int32, (128, width), 0)
    sums = jnp.where(row == 0, gain1_sum / gains[0:1, :], jnp.where(row == 1, gain2[...], 0.0))
    grads_out[:, qkvc + qc :] = jnp.transpose(sums).astype(BF)


def attention_back(blocks, full, cosine, sine, normed, qkv, attended, probs, gain2, heads, ratio):
    local, width = blocks[0].shape
    group = 4 * local
    qc = heads * HD
    shape = jax.ShapeDtypeStruct
    return pl.pallas_call(
        functools.partial(attention_back_kernel, heads, ratio),
        out_shape=(
            shape((group // 2, width), BF),
            shape((group // 2, width), BF),
            shape(full.shape, BF),
        ),
        scratch_shapes=[
            pltpu.VMEM((group, qc), BF),
            pltpu.VMEM((group, qkv.shape[1]), BF),
            pltpu.VMEM((group, width), BF),
        ],
        compiler_params=pltpu.CompilerParams(vmem_limit_bytes=VMEM),
        cost_estimate=CHEAP,
        name="attention_backward",
    )(*blocks, full, cosine, sine, normed, qkv, attended, probs, gain2)


def grad_hidden_kernel(dy, *refs):
    out, wd = refs[-2:]
    units = refs[0].shape[0]
    for n, ref in enumerate(refs[:-2]):
        wd[n * units : (n + 1) * units, :] = ref[...]
    tile = 256
    for m in range(0, dy.shape[0], tile):
        out[m : m + tile, :] = dot(dy[m : m + tile, :], wd[...], ((1,), (1,)))


def grad_hidden_rows(dy, wd):
    wide = len(wd) * wd[0].shape[0]
    return call(
        grad_hidden_kernel,
        jax.ShapeDtypeStruct((dy.shape[0], wide), F32),
        [pltpu.VMEM((wide, dy.shape[1]), BF)],
        "grad_hidden",
        dy,
        *wd,
    )


def units_kernel(mine, far, gate, up, down):
    total = mine[...] + far[...].astype(F32)
    gate[...] = jnp.transpose(total[0])
    up[...] = jnp.transpose(total[1])
    down[...] = total[2]


def expert_kernel(count, *refs):
    x, grad_hidden = refs[:2]
    weights = refs[2 : 2 + 2 * count]
    grad_in, hidden_out, dgate_out, dup_out, wg, wu = refs[2 + 2 * count :]
    units = weights[0].shape[1]

    @pl.when(pl.program_id(0) == 0)
    def _():
        for n in range(count):
            at = slice(n * units, (n + 1) * units)
            wg[:, at] = weights[n][...]
            wu[:, at] = weights[count + n][...]

    gate = jnp.dot(x[...], wg[...], preferred_element_type=F32)
    up = jnp.dot(x[...], wu[...], preferred_element_type=F32)
    sigma = jax.nn.sigmoid(gate)
    silu = gate * sigma
    hidden_out[...] = (silu * up).astype(BF)
    grad_hidden = grad_hidden[...]
    dgate = (grad_hidden * up * sigma * (1.0 + gate * (1.0 - sigma))).astype(BF)
    dup = (grad_hidden * silu).astype(BF)
    dgate_out[...] = dgate
    dup_out[...] = dup
    grad_in[...] = (
        dot(dgate, wg[...], ((1,), (1,))) + dot(dup, wu[...], ((1,), (1,)))
    ).astype(BF)


def expert_layer(x, grad_hidden, wg, wu):
    rows, width = x.shape
    units = wg[0].shape[1]
    count = len(wg)
    wide = count * units
    tile = 256
    shape = jax.ShapeDtypeStruct

    def tiled(columns):
        return pl.BlockSpec((tile, columns), lambda i: (i, 0))

    def whole(array):
        return pl.BlockSpec(array.shape, lambda i: (0, 0))

    weights = list(wg) + list(wu)
    return pl.pallas_call(
        functools.partial(expert_kernel, count),
        grid=(rows // tile,),
        in_specs=[tiled(width), tiled(wide)] + [whole(w) for w in weights],
        out_specs=[tiled(width), tiled(wide), tiled(wide), tiled(wide)],
        out_shape=(
            shape((rows, width), BF),
            shape((rows, wide), BF),
            shape((rows, wide), BF),
            shape((rows, wide), BF),
        ),
        scratch_shapes=[
            pltpu.VMEM((width, wide), BF),
            pltpu.VMEM((width, wide), BF),
        ],
        compiler_params=pltpu.CompilerParams(vmem_limit_bytes=VMEM),
        cost_estimate=COST,
        name="expert_layer",
    )(x, grad_hidden, *weights)


def on_device(
    tokens,
    cotangent,
    norm1_gain,
    w_query,
    w_key,
    w_value,
    w_out,
    norm2_gain,
    expert_gate,
    expert_up,
    expert_down,
    route_gates,
    routes,
    segment,
):
    group = segment.shape[0]
    local, width = tokens.shape
    top_k = routes.shape[1]
    dp_count = lax.axis_size("dp")
    tensor_count = lax.axis_size("tensor")
    experts = expert_gate.shape[0] * dp_count
    capacity = min(group, group * top_k * 5 // (4 * experts))
    share = capacity // tensor_count
    half = dp_count // 2
    slots = half * 2 * share
    four = [0, 2]
    eight = [0, 2, 4, 6]
    parity = lax.axis_index("dp") % 2
    upper = parity == 1
    piece = width // dp_count
    here = lax.axis_index("tensor")
    qc, kc, vc, oc = w_query.shape[1], w_key.shape[1], w_value.shape[1], w_out.shape[1]
    heads = qc // HD
    ratio = qc // kc

    qkvc = qc + kc + vc
    full_shape = (2 * w_query.shape[0], qkvc + oc + 128)
    shard = call(
        shard_kernel,
        jax.ShapeDtypeStruct((w_query.shape[0], full_shape[1]), BF),
        [],
        "weight_shard",
        w_query,
        w_key,
        w_value,
        w_out,
        norm1_gain.reshape(1, -1),
        norm2_gain.reshape(1, -1),
    )
    other = swap(shard, 4)
    parity_ref = parity.reshape(1).astype(jnp.int32)
    spread = pl.pallas_call(
        spread_kernel,
        in_specs=[
            pl.BlockSpec(memory_space=pltpu.SMEM),
            pl.BlockSpec(memory_space=pltpu.VMEM),
            pl.BlockSpec(memory_space=pltpu.VMEM),
        ],
        out_shape=jax.ShapeDtypeStruct((half,) + full_shape, BF),
        compiler_params=pltpu.CompilerParams(vmem_limit_bytes=VMEM),
        name="weight_spread",
    )(parity_ref, shard, other)
    spread, tok, cot, routes, route_gates, segment = lax.optimization_barrier(
        (spread, tokens, cotangent, routes, route_gates, segment)
    )
    full = exchange(spread).reshape(half * full_shape[0], full_shape[1])
    token_blocks = gather_column(tok, four)
    cot_far = [cot] + [swap(cot, mask) for mask in eight[1:]]
    cot_far, own_weights = lax.optimization_barrier(
        (cot_far, [expert_gate[0], expert_up[0], expert_down[0]])
    )
    cot_blocks = cot_far + [swap(block, 1) for block in cot_far]
    far_weights = [swap(w, 2) for w in own_weights]

    order = jnp.array([0, 2, 1, 3], jnp.int32) ^ here
    index = (order[:, None] * local + jnp.arange(local, dtype=jnp.int32)[None, :]).reshape(group)

    def reorder(x):
        split = x.reshape((tensor_count, local) + x.shape[1:])
        return jnp.concatenate(
            [lax.dynamic_index_in_dim(split, here ^ s, 0, False) for s in (0, 2, 1, 3)]
        )

    def pair_up(own, other):
        mid = own.shape[0] // 2
        return jnp.concatenate([own[:mid], other[:mid], own[mid:], other[mid:]])

    seg = reorder(segment)
    route_rows = pair_up(reorder(routes), reorder(swap(routes, 4)))
    gate_rows = pair_up(reorder(route_gates), reorder(swap(route_gates, 4)))
    pair_index = pair_up(index, index)
    pair_group = pair_up(jnp.zeros_like(index), jnp.ones_like(index))

    expert_ids = 2 * jnp.arange(half, dtype=jnp.int32) + parity
    hit = route_rows[None, :, :] == expert_ids[:, None, None]
    mine = pair_group[None, :] == jnp.arange(2, dtype=jnp.int32)[:, None]
    member = (jnp.any(hit, axis=2)[:, None, :] & mine[None]).reshape(2 * half, 2 * group)
    gate_of = jnp.sum(jnp.where(hit, gate_rows[None], 0.0), axis=2)
    gate_of = jnp.broadcast_to(gate_of[:, None, :], (half, 2, 2 * group)).reshape(member.shape)
    before = (pair_index[:, None] < pair_index[None, :]).astype(BF)
    slot = dot(member.astype(BF), before, ((1,), (0,)))
    slot = jnp.where(member, slot, -1.0).astype(jnp.int32)
    wanted = here * share + jnp.arange(share, dtype=jnp.int32)
    place = slot[:, None, :] == wanted[None, :, None]
    slot_gate = jnp.sum(jnp.where(place, gate_of[:, None, :], 0.0), axis=2).reshape(slots)
    place = place.astype(BF).reshape(slots, 2 * group)

    slot_gate = slot_gate.reshape(slots, 1)
    places = doc_positions(seg, index).astype(F32)
    freqs = THETA ** (-(jnp.arange(HD // 2, dtype=F32) * 2.0) / HD)
    angle = places[:, None] * freqs[None, :]
    cosine, sine = jnp.cos(angle), jnp.sin(angle)
    cosine = jnp.concatenate([cosine] * 4, axis=1)
    sine = jnp.concatenate([-sine, sine, -sine, sine], axis=1)
    allowed = (seg[:, None] == seg[None, :]) & (index[:, None] <= index[None, :])
    mask = jnp.where(allowed, 0.0, -1e30).astype(F32)
    grad_packed = pack(place, cot_blocks, slot_gate)
    full, grad_packed = lax.optimization_barrier((full, grad_packed))
    grad_arrived = exchange(grad_packed)
    odd, even, normed1, qkv, attended, probs = attention(
        token_blocks, full, cosine, sine, mask, heads, ratio
    )
    gain1 = full[:, qkvc + oc].astype(F32)
    gain2 = full[:, qkvc + oc + 1].astype(F32)
    odd, even, own_weights, far_weights = lax.optimization_barrier(
        (odd, even, own_weights, far_weights)
    )
    near_weights = [swap(w, 1) for w in own_weights]
    last_weights = [swap(w, 1) for w in far_weights]
    wg, wu, wd = zip(own_weights, far_weights, near_weights, last_weights)
    mixed = tokens.astype(F32) + scatter_column(even, odd, four)

    normal2, inverse2 = rms_forward(mixed)
    normed2 = (normal2 * gain2[None, :]).astype(BF)
    normed2_blocks, held = lax.optimization_barrier(
        (gather_column(normed2, eight), grad_arrived)
    )
    arrived = exchange(pack(place, normed2_blocks, None))

    grad_hidden = grad_hidden_rows(held, wd)
    grad_inputs, hidden, grad_gate_pre, grad_up_pre = expert_layer(
        arrived, grad_hidden, wg, wu
    )
    grad_back = exchange(grad_inputs)
    produced, units_odd, units_even = expert_rest(
        arrived, grad_arrived, hidden, grad_gate_pre, grad_up_pre, wd
    )
    units_got = swap(units_odd, 1)
    count = units_even.shape[1] // 2
    units_mine = units_even[:, :count].astype(F32) + units_got[:, :count].astype(F32)
    units_sent = (
        units_even[:, count:].astype(F32) + units_got[:, count:].astype(F32)
    ).astype(BF)
    grad_back, produced, units_mine, units_sent = lax.optimization_barrier(
        (grad_back, produced, units_mine, units_sent)
    )
    returned = exchange(produced)

    odd, even = combine(place, grad_back, None)
    grad_normed2 = scatter_column(even, odd, eight)
    scaled = grad_normed2 * gain2[None, :]
    inner = jnp.mean(scaled * normal2, axis=1, keepdims=True)
    grad_mixed = cotangent.astype(F32) + inverse2 * (scaled - normal2 * inner)
    gain2_part = jnp.sum(grad_normed2 * normal2, axis=0, keepdims=True)
    grad_branch = gather_column(grad_mixed.astype(BF), four)

    grad_branch, units_sent = lax.optimization_barrier((grad_branch, units_sent))
    units_far = swap(units_sent, 2)

    odd, even, grads = attention_back(
        grad_branch, full, cosine, sine, normed1, qkv, attended, probs, gain2_part, heads, ratio
    )
    odd, even, returned = lax.optimization_barrier((odd, even, returned))
    grad_gate, grad_up, grad_down = call(
        units_kernel,
        (
            jax.ShapeDtypeStruct(expert_gate.shape[1:], F32),
            jax.ShapeDtypeStruct(expert_up.shape[1:], F32),
            jax.ShapeDtypeStruct(expert_down.shape[1:], F32),
        ),
        [],
        "expert_grads",
        units_mine,
        units_far,
    )
    parts = exchange(grads.reshape(half, width // half, grads.shape[1]))
    grad_normed1 = scatter_column(even, odd, four)
    normal1, inverse1 = rms_forward(tokens.astype(F32))
    scaled = grad_normed1 * gain1[None, :]
    inner = jnp.mean(scaled * normal1, axis=1, keepdims=True)
    grad_tokens = grad_mixed + inverse1 * (scaled - normal1 * inner)

    odd, even = combine(place, returned, slot_gate)
    output = mixed + scatter_column(even, odd, eight)
    parts, output, grad_tokens, grad_gate, grad_up, grad_down = lax.optimization_barrier(
        (parts, output, grad_tokens, grad_gate, grad_up, grad_down)
    )
    w_sum, gain_sums = scatter_dp(parts, upper, qkvc + oc)
    own = piece // tensor_count
    gain1_grad = lax.dynamic_slice_in_dim(gain_sums[:, 0], here * own, own, 0)
    gain2_grad = lax.dynamic_slice_in_dim(gain_sums[:, 1], here * own, own, 0)
    return (
        output,
        grad_tokens,
        gain1_grad,
        w_sum[:, :qc],
        w_sum[:, qc : qc + kc],
        w_sum[:, qc + kc : qc + kc + vc],
        w_sum[:, qkvc : qkvc + oc],
        gain2_grad,
        grad_gate[None],
        grad_up[None],
        grad_down[None],
    )


def solution(mesh):
    in_specs = (
        P(("dp", "tensor"), None),
        P(("dp", "tensor"), None),
        P("dp"),
        P("dp", "tensor"),
        P("dp", "tensor"),
        P("dp", "tensor"),
        P("dp", "tensor"),
        P("dp"),
        P("dp", None, "tensor"),
        P("dp", None, "tensor"),
        P("dp", "tensor", None),
        P("dp", None),
        P("dp", None),
        P("dp"),
    )
    out_specs = (
        P(("dp", "tensor"), None),
        P(("dp", "tensor"), None),
        P(("dp", "tensor")),
        P("dp", "tensor"),
        P("dp", "tensor"),
        P("dp", "tensor"),
        P("dp", "tensor"),
        P(("dp", "tensor")),
        P("dp", None, "tensor"),
        P("dp", None, "tensor"),
        P("dp", "tensor", None),
    )
    return jax.shard_map(
        on_device, mesh=mesh, in_specs=in_specs, out_specs=out_specs, check_vma=False
    )
```
